32 devices in a mesh: groups: 2 (over x), seqa: 16 (over z, y, core).
Axes of the slice: x: 2, y: 2, z: 4, core: 2. Of those that a mesh axis runs over, the one named last changes fastest.
Arguments:
- inputs: bfloat16 [4096, 2048], P(('groups', 'seqa')), parts along dimension 0, may hold values from -6 to 6
- gate_in: bfloat16 [4096, 2048], P(('groups', 'seqa')), parts along dimension 0, may hold values from -6 to 6
- grad_out: bfloat16 [4096, 2048], P(('groups', 'seqa')), parts along dimension 0, may hold values from -6 to 6
- right_factor: bfloat16 [128, 128], replicated, may hold values from -0.5 to 0.5
- left_factor: bfloat16 [128, 16, 16], P('seqa'), may hold values from -1.5 to 1.5
Outputs:
- grad_inputs: bfloat16 [4096, 2048], P(('groups', 'seqa')), parts along dimension 0
- grad_gate: bfloat16 [4096, 2048], P(('groups', 'seqa')), parts along dimension 0
- grad_right: float32 [256, 128], P(('groups', 'seqa')), parts along dimension 0
- grad_left: float32 [256, 16, 16], P(('groups', 'seqa')), parts along dimension 0
The draws below stay inside these ranges and needn't reach their ends.
There are 2 independent parts, one for each index of `groups`. The reference program is written for one: setup_inputs(seed, part) draws one part's arguments, and reference() takes and returns one part's arrays. A program takes and returns all parts, laid end to end along the dimension named above; an argument that names none is the same for every part. Nothing has to cross between parts.
All inputs are finite; a program needn't handle non-finite values.
Results may differ from the reference program's by a relative error of at most 0.0058.
Values may be sent and summed in bfloat16 or wider, within the bound.
A program may use at most 64 MiB of HBM per device.

```python
import jax
import jax.numpy as jnp

D = 2048
ROWS = 128
BLOCKS = 16
SEQLEN = 2048


def steps_of(rng, extent, pieces, smallest, largest):
    factor_of = 1.0
    for position, blocks in pieces:
        draws = jax.random.uniform(jax.random.fold_in(jax.random.fold_in(rng, 6), position), (blocks,), jnp.float32, smallest / len(pieces), largest / len(pieces))
        factor_of = factor_of * jnp.repeat(jnp.exp(draws), extent[position] // blocks).reshape((-1,) + (1,) * (len(extent) - 1 - position))
    return factor_of


def gaussian(rng, shape, scale, reach, shards=(), kind=jnp.bfloat16):
    values = jax.random.normal(rng, shape, jnp.float32) * scale
    if len(shards) > 0:
        values = steps_of(rng, shape, shards, -0.22, 0.18) * values
    return jnp.clip(values, min=-reach, max=reach).astype(kind)


def setup_inputs(seed: int = 0, part: int = 0) -> dict:
    keys = jax.random.split(jax.random.key(seed), 6)
    part_splits = jax.random.split(jax.random.fold_in(keys[5], part), 6)
    return {
        "inputs": gaussian(part_splits[0], (SEQLEN, D), 1.0, 6.0, ((0, 16),)),
        "gate_in": gaussian(part_splits[1], (SEQLEN, D), 1.0, 6.0, ((0, 16),)),
        "grad_out": gaussian(part_splits[2], (SEQLEN, D), 1.0, 6.0, ((0, 16),)),
        "right_factor": gaussian(keys[3], (ROWS, ROWS), ROWS ** -0.5, 0.5),
        "left_factor": gaussian(keys[4], (ROWS, BLOCKS, BLOCKS), BLOCKS ** -0.5, 1.5, ((0, 16),)),
    }


def reference(inputs, gate_in, grad_out, right_factor, left_factor):
    places = jnp.arange(ROWS)
    mask_right = (places[:, None] >= places[None, :]).astype(right_factor.dtype)
    right_masked = right_factor * mask_right
    blocks = jnp.arange(BLOCKS)
    mask_left = (blocks[:, None] >= blocks[None, :]).astype(left_factor.dtype)
    left_masked = left_factor * mask_left[None]
    flat = inputs.reshape(BLOCKS, ROWS, D).transpose(1, 0, 2).reshape(ROWS, BLOCKS * D)
    first = jnp.dot(right_masked, flat, preferred_element_type=jnp.float32).astype(jnp.bfloat16)
    first = first.reshape(ROWS, BLOCKS, D)
    second = jnp.einsum("jpa,jad->jpd", left_masked.astype(jnp.float32), first.astype(jnp.float32)).astype(jnp.bfloat16)
    mixed = second.transpose(1, 0, 2).reshape(SEQLEN, D)
    gate_f = gate_in.astype(jnp.float32)
    grad_f = grad_out.astype(jnp.float32)
    sig = jax.nn.sigmoid(gate_f)
    grad_mixed = (grad_f * gate_f * sig).astype(jnp.bfloat16)
    grad_gate = (grad_f * mixed.astype(jnp.float32) * sig * (1.0 + gate_f * (1.0 - sig))).astype(jnp.bfloat16)
    grad_cols = grad_mixed.reshape(BLOCKS, ROWS, D).transpose(1, 0, 2)
    grad_first = jnp.einsum("jpa,jpd->jad", left_masked.astype(jnp.float32), grad_cols.astype(jnp.float32)).astype(jnp.bfloat16)
    grad_left = jnp.einsum("jpd,jad->jpa", grad_cols.astype(jnp.float32), first.astype(jnp.float32)) * mask_left[None].astype(jnp.float32)
    grad_flat = grad_first.reshape(ROWS, BLOCKS * D)
    grad_inputs = jnp.dot(right_masked.T, grad_flat, preferred_element_type=jnp.float32).astype(jnp.bfloat16)
    grad_inputs = grad_inputs.reshape(ROWS, BLOCKS, D).transpose(1, 0, 2).reshape(SEQLEN, D)
    grad_right = jnp.dot(grad_flat, flat.T, preferred_element_type=jnp.float32) * mask_right.astype(jnp.float32)
    return grad_inputs, grad_gate, grad_right, grad_left
```

```python
import functools

import jax
import jax.numpy as jnp
from jax import lax
from jax.experimental import pallas as pl
from jax.experimental.pallas import tpu as pltpu
from jax.sharding import PartitionSpec as P

F32, BF16 = jnp.float32, jnp.bfloat16


def gate_grads(mixed, gate_in, grad_out):
    gate_f = gate_in.astype(jnp.float32)
    grad_f = grad_out.astype(jnp.float32)
    sig = jax.nn.sigmoid(gate_f)
    grad_mixed = (grad_f * gate_f * sig).astype(jnp.bfloat16)
    grad_gate = (grad_f * mixed.astype(jnp.float32) * sig * (1.0 + gate_f * (1.0 - sig))).astype(
        jnp.bfloat16
    )
    return (grad_mixed, grad_gate)


def plain_shards(inputs, gate_in, grad_out, right_factor, left_factor):
    places = jnp.arange(right_factor.shape[0])
    mask_right = (places[:, None] >= places[None, :]).astype(right_factor.dtype)
    right_masked = right_factor * mask_right
    blocks = jnp.arange(left_factor.shape[1])
    mask_left = (blocks[:, None] >= blocks[None, :]).astype(left_factor.dtype)
    left_masked = left_factor * mask_left[None]
    first = jnp.dot(right_masked, inputs, preferred_element_type=jnp.float32).astype(jnp.bfloat16)
    first_cols = lax.all_to_all(first[None], "seqa", split_axis=1, concat_axis=0, tiled=True)
    second = jnp.einsum(
        "jpa,ajd->pjd", left_masked, first_cols, preferred_element_type=jnp.float32
    ).astype(jnp.bfloat16)
    mixed = lax.all_to_all(second, "seqa", split_axis=0, concat_axis=1, tiled=True)[0]
    grad_mixed, grad_gate = gate_grads(mixed, gate_in, grad_out)
    grad_cols = lax.all_to_all(grad_mixed[None], "seqa", split_axis=1, concat_axis=0, tiled=True)
    grad_first_cols = jnp.einsum(
        "jpa,pjd->ajd", left_masked, grad_cols, preferred_element_type=jnp.float32
    ).astype(jnp.bfloat16)
    grad_left = jnp.einsum(
        "pjd,ajd->jpa", grad_cols, first_cols, preferred_element_type=jnp.float32
    ) * mask_left[None].astype(jnp.float32)
    grad_first = lax.all_to_all(grad_first_cols, "seqa", split_axis=0, concat_axis=1, tiled=True)[0]
    grad_inputs = jnp.dot(right_masked.T, grad_first, preferred_element_type=jnp.float32).astype(
        jnp.bfloat16
    )
    mask_float = mask_right.astype(jnp.float32)
    term = lax.dot_general(
        grad_first, inputs, (((1,), (1,)), ((), ())), preferred_element_type=jnp.float32
    )
    grad_right = lax.psum_scatter(term * mask_float, "seqa", scatter_dimension=0, tiled=True)
    return (grad_inputs, grad_gate, grad_right, grad_left)


def iota(shape, dim):
    return lax.broadcasted_iota(jnp.int32, shape, dim)


def dot(a, b, dims=((1,), (0,)), **kw):
    return lax.dot_general(a, b, (dims, ((), ())), preferred_element_type=F32, **kw)


def kernel(
    n, parts, x_ref, gate_ref, gout_ref, right_ref, left_ref,
    gx_ref, ggate_ref, gright_ref, gleft_ref,
    out_buf, in_buf, term_buf, sum_buf, weights, send_sem, recv_sem, tsend_sem, trecv_sem,
):
    me = lax.axis_index("seqa")
    rows, width = x_ref.shape
    r = rows // n
    half = width // 2
    w = half // parts
    barrier = pltpu.get_barrier_semaphore()

    def partner(k):
        return lax.rem(me + k, n)

    @pl.loop(1, n)
    def _(k):
        pl.semaphore_signal(
            barrier, inc=1, device_id={"seqa": partner(k)}, device_id_type=pl.DeviceIdType.MESH
        )

    def copy(kind, part, to):
        return pltpu.make_async_remote_copy(
            src_ref=out_buf.at[kind, part, to],
            dst_ref=in_buf.at[kind, part, me],
            send_sem=send_sem.at[kind, part, to],
            recv_sem=recv_sem.at[kind, part, me],
            device_id={"seqa": to},
            device_id_type=pl.DeviceIdType.MESH,
        )

    def arrival(kind, part, src):
        return pltpu.make_async_remote_copy(
            src_ref=out_buf.at[kind, part, src],
            dst_ref=in_buf.at[kind, part, src],
            send_sem=send_sem.at[kind, part, src],
            recv_sem=recv_sem.at[kind, part, src],
            device_id={"seqa": src},
            device_id_type=pl.DeviceIdType.MESH,
        )

    def send_all(kinds, part):
        @pl.loop(1, n)
        def _(k):
            for kind in kinds:
                copy(kind, part, partner(k)).start()

    def wait_all(kinds, part):
        @pl.loop(1, n)
        def _(k):
            src = lax.rem(me + n - k, n)
            for kind in kinds:
                arrival(kind, part, src).wait_recv()

    def columns(part, h):
        return pl.ds(h * half + part * w, w)

    def pack(v0, v1):
        both = jnp.concatenate([v0.reshape(n, r, w), v1.reshape(n, r, w)], axis=1)
        return both.astype(BF16)

    def unpack(v):
        v = v.astype(F32)
        return v[:, :r].reshape(rows, w), v[:, r:].reshape(rows, w)

    causal = iota((rows, rows), 0) >= iota((rows, rows), 1)
    rm = jnp.where(causal, right_ref[...].astype(F32), 0.0).astype(BF16)

    for part in range(parts):
        vals = [dot(rm, x_ref[:, columns(part, h)]) for h in range(2)]
        out_buf[0, part] = pack(*vals)
        vals = []
        for h in range(2):
            gate = gate_ref[:, columns(part, h)].astype(F32)
            gout = gout_ref[:, columns(part, h)].astype(F32)
            vals.append(gout * gate * jax.nn.sigmoid(gate))
        out_buf[1, part] = pack(*vals)
        if part == 0:
            pl.semaphore_wait(barrier, n - 1)
        send_all((0, 1), part)

    c = n * 2 * r
    row, col = iota((c, n * r), 0), iota((c, n * r), 1)
    pick = (col == (row % r) * n + row // (2 * r)).astype(BF16)
    spread = (iota((n, c), 1) // (2 * r) == iota((n, c), 0)).astype(BF16)
    row, col = iota((c, c), 0), iota((c, c), 1)
    keep = (row % (2 * r) == col % (2 * r)) & (row // (2 * r) >= col // (2 * r))
    wide = dot(dot(pick, left_ref[...]).astype(BF16), spread)
    weights[...] = jnp.where(keep, wide, 0.0).astype(BF16)

    gram = jnp.zeros((c, c), F32)
    for part in range(parts):
        wait_all((0, 1), part)
        for kind in range(2):
            in_buf[kind, part, me] = out_buf[kind, part, me]
        f = in_buf[0, part].reshape(c, w)
        g = in_buf[1, part].reshape(c, w)
        out_buf[2, part] = dot(weights[...], f).astype(BF16).reshape(n, 2 * r, w)
        out_buf[3, part] = dot(weights[...], g, ((0,), (0,))).astype(BF16).reshape(n, 2 * r, w)
        send_all((3, 2), part)
        gram = gram + dot(g, f, ((1,), (1,)))
    gram = jnp.where(keep, gram, 0.0)
    best = lax.Precision.HIGHEST
    narrow = dot(gram, spread.astype(F32), ((1,), (1,)), precision=best)
    gleft_ref[...] = dot(pick.astype(F32), narrow, ((0,), (0,)), precision=best)

    term = jnp.zeros((rows, rows), F32)
    for part in range(parts):
        wait_all((2, 3), part)
        for kind in range(2, 4):
            in_buf[kind, part, me] = out_buf[kind, part, me]
        vals = [v.astype(BF16) for v in unpack(in_buf[3, part])]
        for h in range(2):
            term = term + dot(vals[h], x_ref[:, columns(part, h)], ((1,), (1,)))
        if part == parts - 1:
            term_buf[...] = jnp.where(causal, term, 0.0).reshape(n, r, rows)

            def term_copy(to, slot):
                return pltpu.make_async_remote_copy(
                    src_ref=term_buf.at[to],
                    dst_ref=sum_buf.at[slot],
                    send_sem=tsend_sem.at[to],
                    recv_sem=trecv_sem.at[slot],
                    device_id={"seqa": to},
                    device_id_type=pl.DeviceIdType.MESH,
                )

            @pl.loop(1, n)
            def _(k):
                term_copy(partner(k), me).start()

        for h in range(2):
            gx_ref[:, columns(part, h)] = dot(rm, vals[h], ((0,), (0,))).astype(BF16)
        for h, mixed in enumerate(unpack(in_buf[2, part])):
            gate = gate_ref[:, columns(part, h)].astype(F32)
            gout = gout_ref[:, columns(part, h)].astype(F32)
            sig = jax.nn.sigmoid(gate)
            ggate_ref[:, columns(part, h)] = (
                gout * mixed * sig * (1.0 + gate * (1.0 - sig))
            ).astype(BF16)

    @pl.loop(1, n)
    def _(k):
        src = lax.rem(me + n - k, n)
        term_copy(src, src).wait_recv()

    sum_buf[me] = term_buf[me]
    gright_ref[...] = jnp.sum(sum_buf[...], axis=0)

    @pl.loop(1, n)
    def _(k):
        to = partner(k)
        for part in range(parts):
            for kind in range(4):
                copy(kind, part, to).wait_send()
        term_copy(to, me).wait_send()


def fused_shards(n, parts, inputs, gate_in, grad_out, right_factor, left_factor):
    rows, width = inputs.shape
    r = rows // n
    w = width // 2 // parts
    left2 = left_factor.reshape(r * n, n)
    vmem = pl.BlockSpec(memory_space=pltpu.VMEM)
    gx, gg, gr, gl = pl.pallas_call(
        functools.partial(kernel, n, parts),
        out_shape=(
            jax.ShapeDtypeStruct(inputs.shape, BF16),
            jax.ShapeDtypeStruct(inputs.shape, BF16),
            jax.ShapeDtypeStruct((r, rows), F32),
            jax.ShapeDtypeStruct((r * n, n), F32),
        ),
        in_specs=[vmem] * 5,
        out_specs=(vmem,) * 4,
        scratch_shapes=[
            pltpu.VMEM((4, parts, n, 2 * r, w), BF16),
            pltpu.VMEM((4, parts, n, 2 * r, w), BF16),
            pltpu.VMEM((n, r, rows), F32),
            pltpu.VMEM((n, r, rows), F32),
            pltpu.VMEM((2 * r * n, 2 * r * n), BF16),
            pltpu.SemaphoreType.DMA((4, parts, n)),
            pltpu.SemaphoreType.DMA((4, parts, n)),
            pltpu.SemaphoreType.DMA((n,)),
            pltpu.SemaphoreType.DMA((n,)),
        ],
        compiler_params=pltpu.CompilerParams(
            collective_id=0, has_side_effects=True, vmem_limit_bytes=40 * 2**20
        ),
    )(inputs, gate_in, grad_out, right_factor, left2)
    return gx, gg, gr, gl.reshape(r, n, n)


def solution(mesh):
    n = mesh.shape["seqa"]

    def shards(inputs, gate_in, grad_out, right_factor, left_factor):
        rows = inputs.shape[0]
        if rows == 8 * n and left_factor.shape == (8, n, n):
            return fused_shards(n, 2, inputs, gate_in, grad_out, right_factor, left_factor)
        return plain_shards(inputs, gate_in, grad_out, right_factor, left_factor)

    in_specs = (
        P(("groups", "seqa"), None),
        P(("groups", "seqa"), None),
        P(("groups", "seqa"), None),
        P(),
        P("seqa", None, None),
    )
    out_specs = (
        P(("groups", "seqa"), None),
        P(("groups", "seqa"), None),
        P(("groups", "seqa"), None),
        P(("groups", "seqa"), None, None),
    )
    return jax.shard_map(shards, mesh=mesh, in_specs=in_specs, out_specs=out_specs, check_vma=False)
```

```python
import functools

import jax
import jax.numpy as jnp
from jax import lax
from jax.experimental import pallas as pl
from jax.experimental.pallas import tpu as pltpu
from jax.sharding import PartitionSpec as P

F32, BF16 = jnp.float32, jnp.bfloat16
PARTS = 4
SUMS = F32


def gate_grads(mixed, gate_in, grad_out):
    gate_f = gate_in.astype(jnp.float32)
    grad_f = grad_out.astype(jnp.float32)
    sig = jax.nn.sigmoid(gate_f)
    grad_mixed = (grad_f * gate_f * sig).astype(jnp.bfloat16)
    grad_gate = (grad_f * mixed.astype(jnp.float32) * sig * (1.0 + gate_f * (1.0 - sig))).astype(
        jnp.bfloat16
    )
    return (grad_mixed, grad_gate)


def plain_shards(inputs, gate_in, grad_out, right_factor, left_factor):
    places = jnp.arange(right_factor.shape[0])
    mask_right = (places[:, None] >= places[None, :]).astype(right_factor.dtype)
    right_masked = right_factor * mask_right
    blocks = jnp.arange(left_factor.shape[1])
    mask_left = (blocks[:, None] >= blocks[None, :]).astype(left_factor.dtype)
    left_masked = left_factor * mask_left[None]
    first = jnp.dot(right_masked, inputs, preferred_element_type=jnp.float32).astype(jnp.bfloat16)
    first_cols = lax.all_to_all(first[None], "seqa", split_axis=1, concat_axis=0, tiled=True)
    second = jnp.einsum(
        "jpa,ajd->pjd", left_masked, first_cols, preferred_element_type=jnp.float32
    ).astype(jnp.bfloat16)
    mixed = lax.all_to_all(second, "seqa", split_axis=0, concat_axis=1, tiled=True)[0]
    grad_mixed, grad_gate = gate_grads(mixed, gate_in, grad_out)
    grad_cols = lax.all_to_all(grad_mixed[None], "seqa", split_axis=1, concat_axis=0, tiled=True)
    grad_first_cols = jnp.einsum(
        "jpa,pjd->ajd", left_masked, grad_cols, preferred_element_type=jnp.float32
    ).astype(jnp.bfloat16)
    grad_left = jnp.einsum(
        "pjd,ajd->jpa", grad_cols, first_cols, preferred_element_type=jnp.float32
    ) * mask_left[None].astype(jnp.float32)
    grad_first = lax.all_to_all(grad_first_cols, "seqa", split_axis=0, concat_axis=1, tiled=True)[0]
    grad_inputs = jnp.dot(right_masked.T, grad_first, preferred_element_type=jnp.float32).astype(
        jnp.bfloat16
    )
    mask_float = mask_right.astype(jnp.float32)
    term = lax.dot_general(
        grad_first, inputs, (((1,), (1,)), ((), ())), preferred_element_type=jnp.float32
    )
    grad_right = lax.psum_scatter(term * mask_float, "seqa", scatter_dimension=0, tiled=True)
    return (grad_inputs, grad_gate, grad_right, grad_left)


def iota(shape, dim):
    return lax.broadcasted_iota(jnp.int32, shape, dim)


def dot(a, b, dims=((1,), (0,)), **kw):
    return lax.dot_general(a, b, (dims, ((), ())), preferred_element_type=F32, **kw)


PLANES = 4
PEERS = 4


def kernel(
    parts, x_hbm, gate_hbm, gout_hbm, right_hbm, left_hbm,
    gx_ref, ggate_ref, gright_ref, gleft_ref,
    x_ref, gate_ref, gout_ref, right_ref, left_ref,
    cols_out, cols, back_out, back_in, sums_out, sums_in, weights, gram, term,
    left_out, left_in, gl_out, gl_in, term_out, term_in,
    load_sem, a_send, a_recv, relay_send, relay_recv, sum_send, sum_recv, b_send, b_recv,
    left_send, left_recv, gl_send, gl_recv, t_send, t_recv,
):
    n = PLANES * PEERS
    me = lax.axis_index("seqa")
    z, i = me // PEERS, me % PEERS
    rows, width = x_ref.shape
    jj = rows // PEERS
    w = width // parts
    m = PEERS * jj
    barrier = pltpu.get_barrier_semaphore()

    def remote(src, dst, send, recv, to):
        return pltpu.make_async_remote_copy(
            src_ref=src, dst_ref=dst, send_sem=send, recv_sem=recv,
            device_id={"seqa": to}, device_id_type=pl.DeviceIdType.MESH,
        )

    @pl.loop(1, n)
    def _(k):
        pl.semaphore_signal(
            barrier, inc=1, device_id={"seqa": lax.rem(me + k, n)},
            device_id_type=pl.DeviceIdType.MESH,
        )

    pairs = (
        (x_hbm, x_ref), (right_hbm, right_ref), (gate_hbm, gate_ref),
        (gout_hbm, gout_ref), (left_hbm, left_ref),
    )
    loads = [pltpu.make_async_copy(a, b, load_sem.at[k]) for k, (a, b) in enumerate(pairs)]
    for load in loads:
        load.start()

    def columns(c):
        return pl.ds(pl.multiple_of(c * w, w), w)

    causal = iota((rows, rows), 0) >= iota((rows, rows), 1)

    def rm():
        return jnp.where(causal, right_ref[...].astype(F32), 0.0).astype(BF16)

    def block(kind, c, q):
        return cols.at[kind, c, pl.ds(PEERS * q, PEERS)]

    def planes(kind, c, lo, hi):
        return cols[kind, c, PEERS * lo : PEERS * hi].reshape((hi - lo) * m, w)

    def w_block(p0, p1, q0, q1):
        return weights[m * p0 : m * p1, m * q0 : m * q1]

    def a_copy(kind, c, p):
        return remote(
            cols_out.at[kind, c, p], cols.at[kind, c, me],
            a_send.at[kind, c, p], a_recv.at[kind, c, i], PEERS * z + p,
        )

    def a_arrival(kind, c, p):
        return remote(
            cols_out.at[kind, c, p], cols.at[kind, c, PEERS * z + p],
            a_send.at[kind, c, p], a_recv.at[kind, c, p], PEERS * z + p,
        )

    def compute_a(c):
        first = dot(rm(), x_ref[:, columns(c)])
        cols_out[0, c] = first.astype(BF16).reshape(PEERS, jj, w)
        gate = gate_ref[:, columns(c)].astype(F32)
        gout = gout_ref[:, columns(c)].astype(F32)
        mixed_grad = gout * gate * jax.nn.sigmoid(gate)
        cols_out[1, c] = mixed_grad.astype(BF16).reshape(PEERS, jj, w)

    def send_a(c):
        for k in range(1, PEERS):
            for kind in range(2):
                a_copy(kind, c, lax.rem(i + k, PEERS)).start()
        for kind in range(2):
            cols[kind, c, me] = cols_out[kind, c, i]

    relays = {0: (0, (1, 2)), 1: (0, (2,)), 2: (1, (1,)), 3: (1, (2, 1))}

    def relay(kind, c, q, slot, to_plane):
        return remote(
            block(kind, c, q), block(kind, c, q),
            relay_send.at[c, slot], relay_recv.at[kind, c, q], PEERS * to_plane + i,
        )

    def sums(c, to_plane):
        return remote(
            sums_out.at[c], sums_in.at[c], sum_send.at[c], sum_recv.at[c], PEERS * to_plane + i
        )

    def b_copy(kind, c, p, slot):
        return remote(
            back_out.at[kind, c, p], back_in.at[kind, c, slot],
            b_send.at[kind, c, p], b_recv.at[kind, c, slot], PEERS * z + p,
        )

    def send_back(kind, c, value):
        back_out[kind, c] = value.astype(BF16).reshape(PEERS, jj, w)
        for k in range(1, PEERS):
            b_copy(kind, c, lax.rem(i + k, PEERS), i).start()
        back_in[kind, c, i] = back_out[kind, c, i]

    def add_gram(c, p0, p1, q0, q1):
        gram[m * p0 : m * p1, m * q0 : m * q1] += dot(
            planes(1, c, p0, p1), planes(0, c, q0, q1), ((1,), (1,))
        )

    def stage_b(c):
        for k in range(1, PEERS):
            for kind in range(2):
                a_arrival(kind, c, lax.rem(i + PEERS - k, PEERS)).wait_recv()
        for q, (kind, targets) in relays.items():

            @pl.when(z == q)
            def _(q=q, kind=kind, targets=targets):
                for slot, to_plane in enumerate(targets):
                    relay(kind, c, q, slot, to_plane).start()
                if q == 0:
                    send_back(0, c, dot(w_block(0, 1, 0, 1), planes(0, c, 0, 1)))
                    add_gram(c, 0, 1, 0, 1)
                if q == 3:
                    send_back(1, c, dot(w_block(3, 4, 3, 4), planes(1, c, 3, 4), ((0,), (0,))))
                    add_gram(c, 3, 4, 3, 4)

    def stage_d(c):
        @pl.when(z == 1)
        def _():
            relay(0, c, 0, 0, 0).wait_recv()
            send_back(0, c, dot(w_block(1, 2, 0, 2), planes(0, c, 0, 2)))
            relay(1, c, 2, 0, 2).wait_recv()
            relay(1, c, 3, 0, 3).wait_recv()
            g = planes(1, c, 1, 4)
            sums_out[c] = dot(w_block(1, 4, 0, 1), g, ((0,), (0,))).reshape(PEERS, jj, w)
            sums(c, 0).start()
            send_back(1, c, dot(w_block(1, 4, 1, 2), g, ((0,), (0,))))
            add_gram(c, 1, 4, 0, 1)
            add_gram(c, 1, 2, 1, 2)

        @pl.when(z == 2)
        def _():
            relay(1, c, 3, 0, 3).wait_recv()
            send_back(1, c, dot(w_block(2, 4, 2, 3), planes(1, c, 2, 4), ((0,), (0,))))
            relay(0, c, 1, 0, 1).wait_recv()
            relay(0, c, 0, 0, 0).wait_recv()
            f = planes(0, c, 0, 3)
            sums_out[c] = dot(w_block(3, 4, 0, 3), f).reshape(PEERS, jj, w)
            sums(c, 3).start()
            send_back(0, c, dot(w_block(2, 3, 0, 3), f))
            add_gram(c, 2, 4, 1, 3)

    def stage_s(c):
        @pl.when(z == 0)
        def _():
            own = dot(w_block(0, 1, 0, 1), planes(1, c, 0, 1), ((0,), (0,)))
            sums(c, 1).wait_recv()
            send_back(1, c, own + sums_in[c].reshape(m, w))

        @pl.when(z == 3)
        def _():
            own = dot(w_block(3, 4, 3, 4), planes(0, c, 3, 4))
            sums(c, 2).wait_recv()
            send_back(0, c, own + sums_in[c].reshape(m, w))

    def term_copy(to, slot):
        return remote(term_out.at[to], term_in.at[slot], t_send.at[to], t_recv.at[slot], to)

    def stage_e(c):
        for k in range(1, PEERS):
            p = lax.rem(i + PEERS - k, PEERS)
            for kind in range(2):
                b_copy(kind, c, p, p).wait_recv()
        grad_first = back_in[1, c].reshape(rows, w)
        term[...] += dot(grad_first, x_ref[:, columns(c)], ((1,), (1,)))

        @pl.when(c == parts - 1)
        def _():
            term_out[...] = jnp.where(causal, term[...], 0.0).reshape(n, rows // n, rows)

            @pl.loop(1, n)
            def _(k):
                term_copy(lax.rem(me + k, n), me).start()

        gx_ref[:, columns(c)] = dot(rm(), grad_first, ((0,), (0,))).astype(BF16)
        mixed = back_in[0, c].reshape(rows, w).astype(F32)
        gate = gate_ref[:, columns(c)].astype(F32)
        gout = gout_ref[:, columns(c)].astype(F32)
        sig = jax.nn.sigmoid(gate)
        ggate_ref[:, columns(c)] = (gout * mixed * sig * (1.0 + gate * (1.0 - sig))).astype(BF16)

    def left_copy(to, slot):
        return remote(left_out, left_in.at[slot], left_send.at[to // PEERS], left_recv.at[slot], to)

    def gl_copy(to_slot, to, slot):
        return remote(
            gl_out.at[to_slot], gl_in.at[slot], gl_send.at[to_slot], gl_recv.at[slot], to
        )

    for load in loads:
        load.wait()
    compute_a(0)
    eye = (iota((rows, rows), 0) == iota((rows, rows), 1)).astype(BF16)
    left_out[...] = dot(left_ref[...], eye, ((0,), (0,))).astype(BF16)
    pl.semaphore_wait(barrier, n - 1)
    for plane in range(PLANES):
        to = PEERS * plane + z

        @pl.when(to != me)
        def _(to=to):
            left_copy(to, i).start()

        @pl.when(to == me)
        def _():
            left_in[i] = left_out[...]

    send_a(0)
    if parts > 1:
        compute_a(1)
        send_a(1)
    gram[...] = jnp.zeros_like(gram)
    term[...] = jnp.zeros_like(term)

    size = n * jj

    def pick():
        row, col = iota((size, size), 0), iota((size, size), 1)
        return col == (row % jj) * n + row // jj

    def spread():
        return iota((n, size), 1) // jj == iota((n, size), 0)

    def keep():
        row, col = iota((size, size), 0), iota((size, size), 1)
        return (row % jj == col % jj) & (row // jj >= col // jj)

    for s in range(PEERS):
        src = PEERS * i + s

        @pl.when(src != me)
        def _(src=src, s=s):
            left_copy(src, s).wait_recv()

    left_all = jnp.concatenate([left_in[s] for s in range(PEERS)], axis=1)
    picked = dot(pick().astype(BF16), left_all, ((1,), (1,))).astype(BF16)
    weights[...] = jnp.where(keep(), dot(picked, spread().astype(BF16)), 0.0).astype(BF16)

    def left_grads():
        best = lax.Precision.HIGHEST
        summed = dot(
            jnp.where(keep(), gram[...], 0.0), spread().astype(F32), ((1,), (1,)), precision=best
        )
        flat = dot(summed, pick().astype(F32), ((0,), (0,)), precision=best)
        each = size // PEERS
        for s in range(PEERS):
            gl_out[s] = flat[:, s * each : (s + 1) * each]
            to = PEERS * i + s

            @pl.when(to != me)
            def _(to=to, s=s):
                gl_copy(s, to, z).start()

            @pl.when(to == me)
            def _(s=s):
                gl_in[z] = gl_out[s]

    def at(cond, stage, c):
        @pl.when(cond)
        def _():
            stage(c)

    def a_part(c):
        compute_a(c)
        send_a(c)

    @pl.loop(0, parts + 3)
    def _(t):
        at(t < parts, stage_b, t)
        at(t < parts - 2, a_part, t + 2)
        at((t >= 1) & (t <= parts), stage_d, t - 1)
        at((t >= 2) & (t <= parts + 1), stage_s, t - 2)

        @pl.when(t == parts)
        def _():
            left_grads()

        at(t >= 3, stage_e, t - 3)

    for plane in range(PLANES):
        src = PEERS * plane + z

        @pl.when(src != me)
        def _(src=src, plane=plane):
            gl_copy(0, src, plane).wait_recv()

    total = gl_in[0] + gl_in[1] + gl_in[2] + gl_in[3]
    gleft_ref[...] = total.T

    @pl.loop(1, n)
    def _(k):
        src = lax.rem(me + n - k, n)
        term_copy(src, src).wait_recv()

    term_in[me] = term_out[me]
    gright_ref[...] = jnp.sum(term_in[...], axis=0)

    @pl.loop(0, parts)
    def _(c):
        for k in range(1, PEERS):
            p = lax.rem(i + k, PEERS)
            for kind in range(2):
                a_copy(kind, c, p).wait_send()
                b_copy(kind, c, p, i).wait_send()
        for q, (kind, targets) in relays.items():

            @pl.when(z == q)
            def _(q=q, kind=kind, targets=targets):
                for slot, to_plane in enumerate(targets):
                    relay(kind, c, q, slot, to_plane).wait_send()

        @pl.when((z == 1) | (z == 2))
        def _():
            sums(c, 0).wait_send()

    for plane in range(PLANES):
        to = PEERS * plane + z

        @pl.when(to != me)
        def _(to=to):
            left_copy(to, i).wait_send()

    for s in range(PEERS):
        to = PEERS * i + s

        @pl.when(to != me)
        def _(to=to, s=s):
            gl_copy(s, to, z).wait_send()

    @pl.loop(1, n)
    def _(k):
        term_copy(lax.rem(me + k, n), me).wait_send()


def fused_shards(parts, inputs, gate_in, grad_out, right_factor, left_factor):
    rows, width = inputs.shape
    n = PLANES * PEERS
    r, jj, w = rows // n, rows // PEERS, width // parts
    left2 = left_factor.reshape(r * n, n)
    vmem = pl.BlockSpec(memory_space=pltpu.VMEM)
    hbm = pl.BlockSpec(memory_space=pl.ANY)
    dma = pltpu.SemaphoreType.DMA
    gx, gg, gr, gl = pl.pallas_call(
        functools.partial(kernel, parts),
        out_shape=(
            jax.ShapeDtypeStruct(inputs.shape, BF16),
            jax.ShapeDtypeStruct(inputs.shape, BF16),
            jax.ShapeDtypeStruct((r, rows), F32),
            jax.ShapeDtypeStruct((r * n, n), F32),
        ),
        in_specs=[hbm] * 5,
        out_specs=(vmem,) * 4,
        scratch_shapes=[
            pltpu.VMEM(inputs.shape, BF16),
            pltpu.VMEM(inputs.shape, BF16),
            pltpu.VMEM(inputs.shape, BF16),
            pltpu.VMEM(right_factor.shape, BF16),
            pltpu.VMEM(left2.shape, BF16),
            pltpu.VMEM((2, parts, PEERS, jj, w), BF16),
            pltpu.VMEM((2, parts, n, jj, w), BF16),
            pltpu.VMEM((2, parts, PEERS, jj, w), BF16),
            pltpu.VMEM((2, parts, PEERS, jj, w), BF16),
            pltpu.VMEM((parts, PEERS, jj, w), SUMS),
            pltpu.VMEM((parts, PEERS, jj, w), SUMS),
            pltpu.VMEM((n * jj, n * jj), BF16),
            pltpu.VMEM((n * jj, n * jj), F32),
            pltpu.VMEM((rows, rows), F32),
            pltpu.VMEM((n, r * n), BF16),
            pltpu.VMEM((PEERS, n, r * n), BF16),
            pltpu.VMEM((PEERS, n, r * n), F32),
            pltpu.VMEM((PLANES, n, r * n), F32),
            pltpu.VMEM((n, r, rows), F32),
            pltpu.VMEM((n, r, rows), F32),
            dma((5,)),
            dma((2, parts, PEERS)),
            dma((2, parts, PEERS)),
            dma((parts, 2)),
            dma((2, parts, PLANES)),
            dma((parts,)),
            dma((parts,)),
            dma((2, parts, PEERS)),
            dma((2, parts, PEERS)),
            dma((PLANES,)),
            dma((PEERS,)),
            dma((PEERS,)),
            dma((PLANES,)),
            dma((n,)),
            dma((n,)),
        ],
        compiler_params=pltpu.CompilerParams(
            collective_id=0, has_side_effects=True, vmem_limit_bytes=56 * 2**20
        ),
    )(inputs, gate_in, grad_out, right_factor, left2)
    return gx, gg, gr, gl.reshape(r, n, n)


def solution(mesh):
    n = mesh.shape["seqa"]

    def shards(inputs, gate_in, grad_out, right_factor, left_factor):
        rows = inputs.shape[0]
        if n == PLANES * PEERS and rows == 128 and left_factor.shape == (8, n, n):
            return fused_shards(PARTS, inputs, gate_in, grad_out, right_factor, left_factor)
        return plain_shards(inputs, gate_in, grad_out, right_factor, left_factor)

    in_specs = (
        P(("groups", "seqa"), None),
        P(("groups", "seqa"), None),
        P(("groups", "seqa"), None),
        P(),
        P("seqa", None, None),
    )
    out_specs = (
        P(("groups", "seqa"), None),
        P(("groups", "seqa"), None),
        P(("groups", "seqa"), None),
        P(("groups", "seqa"), None, None),
    )
    return jax.shard_map(shards, mesh=mesh, in_specs=in_specs, out_specs=out_specs, check_vma=False)
```

```python
import functools

import jax
import jax.numpy as jnp
from jax import lax
from jax.experimental import pallas as pl
from jax.experimental.pallas import tpu as pltpu
from jax.sharding import PartitionSpec as P

F32, BF16 = jnp.float32, jnp.bfloat16
PARTS = 8
SUMS = BF16


def gate_grads(mixed, gate_in, grad_out):
    gate_f = gate_in.astype(jnp.float32)
    grad_f = grad_out.astype(jnp.float32)
    sig = jax.nn.sigmoid(gate_f)
    grad_mixed = (grad_f * gate_f * sig).astype(jnp.bfloat16)
    grad_gate = (grad_f * mixed.astype(jnp.float32) * sig * (1.0 + gate_f * (1.0 - sig))).astype(
        jnp.bfloat16
    )
    return (grad_mixed, grad_gate)


def plain_shards(inputs, gate_in, grad_out, right_factor, left_factor):
    places = jnp.arange(right_factor.shape[0])
    mask_right = (places[:, None] >= places[None, :]).astype(right_factor.dtype)
    right_masked = right_factor * mask_right
    blocks = jnp.arange(left_factor.shape[1])
    mask_left = (blocks[:, None] >= blocks[None, :]).astype(left_factor.dtype)
    left_masked = left_factor * mask_left[None]
    first = jnp.dot(right_masked, inputs, preferred_element_type=jnp.float32).astype(jnp.bfloat16)
    first_cols = lax.all_to_all(first[None], "seqa", split_axis=1, concat_axis=0, tiled=True)
    second = jnp.einsum(
        "jpa,ajd->pjd", left_masked, first_cols, preferred_element_type=jnp.float32
    ).astype(jnp.bfloat16)
    mixed = lax.all_to_all(second, "seqa", split_axis=0, concat_axis=1, tiled=True)[0]
    grad_mixed, grad_gate = gate_grads(mixed, gate_in, grad_out)
    grad_cols = lax.all_to_all(grad_mixed[None], "seqa", split_axis=1, concat_axis=0, tiled=True)
    grad_first_cols = jnp.einsum(
        "jpa,pjd->ajd", left_masked, grad_cols, preferred_element_type=jnp.float32
    ).astype(jnp.bfloat16)
    grad_left = jnp.einsum(
        "pjd,ajd->jpa", grad_cols, first_cols, preferred_element_type=jnp.float32
    ) * mask_left[None].astype(jnp.float32)
    grad_first = lax.all_to_all(grad_first_cols, "seqa", split_axis=0, concat_axis=1, tiled=True)[0]
    grad_inputs = jnp.dot(right_masked.T, grad_first, preferred_element_type=jnp.float32).astype(
        jnp.bfloat16
    )
    mask_float = mask_right.astype(jnp.float32)
    term = lax.dot_general(
        grad_first, inputs, (((1,), (1,)), ((), ())), preferred_element_type=jnp.float32
    )
    grad_right = lax.psum_scatter(term * mask_float, "seqa", scatter_dimension=0, tiled=True)
    return (grad_inputs, grad_gate, grad_right, grad_left)


AHEAD = 2


def iota(shape, dim):
    return lax.broadcasted_iota(jnp.int32, shape, dim)


def dot(a, b, dims=((1,), (0,)), **kw):
    return lax.dot_general(a, b, (dims, ((), ())), preferred_element_type=F32, **kw)


PLANES = 4
PEERS = 4


def kernel(
    parts, x_hbm, gate_hbm, gout_hbm, right_hbm, left_hbm,
    gx_ref, ggate_ref, gright_ref, gleft_ref,
    x_ref, gate_ref, gout_ref, right_ref, left_ref,
    cols_out, cols, back_out, back_in, sums_out, sums_in, weights, weights_t, rights, gram, term,
    left_out, left_in, gl_out, gl_in, term_out, term_in,
    load_sem, a_send, a_recv, relay_send, relay_recv, sum_send, sum_recv, b_send, b_recv,
    left_send, left_recv, gl_send, gl_recv, t_send, t_recv,
):
    n = PLANES * PEERS
    me = lax.axis_index("seqa")
    z, i = me // PEERS, me % PEERS
    rows, width = x_ref.shape
    jj = rows // PEERS
    w = width // parts
    m = PEERS * jj
    barrier = pltpu.get_barrier_semaphore()

    def remote(src, dst, send, recv, to):
        return pltpu.make_async_remote_copy(
            src_ref=src, dst_ref=dst, send_sem=send, recv_sem=recv,
            device_id={"seqa": to}, device_id_type=pl.DeviceIdType.MESH,
        )

    @pl.loop(1, n)
    def _(k):
        pl.semaphore_signal(
            barrier, inc=1, device_id={"seqa": lax.rem(me + k, n)},
            device_id_type=pl.DeviceIdType.MESH,
        )

    pairs = (
        (x_hbm, x_ref), (right_hbm, right_ref), (gate_hbm, gate_ref),
        (gout_hbm, gout_ref), (left_hbm, left_ref),
    )
    loads = [pltpu.make_async_copy(a, b, load_sem.at[k]) for k, (a, b) in enumerate(pairs)]
    for load in loads:
        load.start()

    def columns(c):
        return pl.ds(pl.multiple_of(c * w, w), w)

    causal = iota((rows, rows), 0) >= iota((rows, rows), 1)


    def block(kind, c, q):
        return cols.at[kind, c, pl.ds(PEERS * q, PEERS)]

    def planes(kind, c, lo, hi):
        return cols[kind, c, PEERS * lo : PEERS * hi].reshape((hi - lo) * m, w)

    def wt_block(q0, q1, p0, p1):
        return weights_t[m * q0 : m * q1, m * p0 : m * p1]

    def w_block(p0, p1, q0, q1):
        return weights[m * p0 : m * p1, m * q0 : m * q1]

    def a_copy(kind, c, p):
        return remote(
            cols_out.at[kind, c, p], cols.at[kind, c, me],
            a_send.at[kind, c, p], a_recv.at[kind, c, i], PEERS * z + p,
        )

    def a_arrival(kind, c, p):
        return remote(
            cols_out.at[kind, c, p], cols.at[kind, c, PEERS * z + p],
            a_send.at[kind, c, p], a_recv.at[kind, c, p], PEERS * z + p,
        )

    def compute_a(c):
        first = dot(rights[0], x_ref[:, columns(c)])
        cols_out[0, c] = first.astype(BF16).reshape(PEERS, jj, w)
        gate = gate_ref[:, columns(c)].astype(F32)
        gout = gout_ref[:, columns(c)].astype(F32)
        mixed_grad = gout * gate * jax.nn.sigmoid(gate)
        cols_out[1, c] = mixed_grad.astype(BF16).reshape(PEERS, jj, w)
        for kind in range(2):
            cols[kind, c, me] = cols_out[kind, c, i]

    def send_a(c):
        for k in range(1, PEERS):
            for kind in range(2):
                a_copy(kind, c, lax.rem(i + k, PEERS)).start()

    relays = {0: (0, (2, 1)), 1: (0, (2,)), 2: (1, (1,)), 3: (1, (1, 2))}

    def relay(kind, c, q, slot, to_plane):
        return remote(
            block(kind, c, q), block(kind, c, q),
            relay_send.at[c, slot], relay_recv.at[kind, c, q], PEERS * to_plane + i,
        )

    def sums(c, to_plane):
        return remote(
            sums_out.at[c], sums_in.at[c], sum_send.at[c], sum_recv.at[c], PEERS * to_plane + i
        )

    def b_copy(kind, c, p, slot):
        return remote(
            back_out.at[kind, c, p], back_in.at[kind, c, slot],
            b_send.at[kind, c, p], b_recv.at[kind, c, slot], PEERS * z + p,
        )

    def send_back(kind, c, value):
        back_out[kind, c] = value.astype(BF16).reshape(PEERS, jj, w)
        for k in range(1, PEERS):
            b_copy(kind, c, lax.rem(i + k, PEERS), i).start()
        back_in[kind, c, i] = back_out[kind, c, i]

    def add_gram(c, p0, p1, q0, q1):
        gram[m * p0 : m * p1, m * q0 : m * q1] += dot(
            planes(1, c, p0, p1), planes(0, c, q0, q1), ((1,), (1,))
        )

    def start_relays(c):
        for k in range(1, PEERS):
            for kind in range(2):
                a_arrival(kind, c, lax.rem(i + PEERS - k, PEERS)).wait_recv()
        for q, (kind, targets) in relays.items():

            @pl.when(z == q)
            def _(q=q, kind=kind, targets=targets):
                for slot, to_plane in enumerate(targets):
                    relay(kind, c, q, slot, to_plane).start()

    def stage_b(c):
        @pl.when(z == 0)
        def _():
            send_back(0, c, dot(w_block(0, 1, 0, 1), planes(0, c, 0, 1)))
            add_gram(c, 0, 1, 0, 1)

        @pl.when(z == 3)
        def _():
            send_back(1, c, dot(wt_block(3, 4, 3, 4), planes(1, c, 3, 4)))
            add_gram(c, 3, 4, 3, 4)

    def stage_d(c):
        @pl.when(z == 1)
        def _():
            relay(0, c, 0, 0, 0).wait_recv()
            send_back(0, c, dot(w_block(1, 2, 0, 2), planes(0, c, 0, 2)))
            relay(1, c, 2, 0, 2).wait_recv()
            relay(1, c, 3, 0, 3).wait_recv()
            g = planes(1, c, 1, 4)
            summed = dot(wt_block(0, 1, 1, 4), g)
            sums_out[c] = summed.astype(SUMS).reshape(PEERS, jj, w)
            sums(c, 0).start()
            send_back(1, c, dot(wt_block(1, 2, 1, 4), g))
            add_gram(c, 1, 4, 0, 1)
            add_gram(c, 1, 2, 1, 2)

        @pl.when(z == 2)
        def _():
            relay(1, c, 3, 0, 3).wait_recv()
            send_back(1, c, dot(wt_block(2, 3, 2, 4), planes(1, c, 2, 4)))
            relay(0, c, 1, 0, 1).wait_recv()
            relay(0, c, 0, 0, 0).wait_recv()
            f = planes(0, c, 0, 3)
            sums_out[c] = dot(w_block(3, 4, 0, 3), f).astype(SUMS).reshape(PEERS, jj, w)
            sums(c, 3).start()
            send_back(0, c, dot(w_block(2, 3, 0, 3), f))
            add_gram(c, 2, 4, 1, 3)

    def stage_s(c):
        @pl.when(z == 0)
        def _():
            own = dot(wt_block(0, 1, 0, 1), planes(1, c, 0, 1))
            sums(c, 1).wait_recv()
            send_back(1, c, own + sums_in[c].reshape(m, w))

        @pl.when(z == 3)
        def _():
            own = dot(w_block(3, 4, 3, 4), planes(0, c, 3, 4))
            sums(c, 2).wait_recv()
            send_back(0, c, own + sums_in[c].reshape(m, w))

    def term_copy(to, slot):
        return remote(term_out.at[to], term_in.at[slot], t_send.at[to], t_recv.at[slot], to)

    def stage_e(c):
        for k in range(1, PEERS):
            p = lax.rem(i + PEERS - k, PEERS)
            for kind in range(2):
                b_copy(kind, c, p, p).wait_recv()
        grad_first = back_in[1, c].reshape(rows, w)
        term[...] += dot(grad_first, x_ref[:, columns(c)], ((1,), (1,)))

        @pl.when(c == parts - 1)
        def _():
            term_out[...] = jnp.where(causal, term[...], 0.0).reshape(n, rows // n, rows)

            @pl.loop(1, n)
            def _(k):
                term_copy(lax.rem(me + k, n), me).start()

        gx_ref[:, columns(c)] = dot(rights[1], grad_first).astype(BF16)
        mixed = back_in[0, c].reshape(rows, w).astype(F32)
        gate = gate_ref[:, columns(c)].astype(F32)
        gout = gout_ref[:, columns(c)].astype(F32)
        sig = jax.nn.sigmoid(gate)
        ggate_ref[:, columns(c)] = (gout * mixed * sig * (1.0 + gate * (1.0 - sig))).astype(BF16)

    def left_copy(to, slot):
        return remote(left_out, left_in.at[slot], left_send.at[to // PEERS], left_recv.at[slot], to)

    def gl_copy(to_slot, to, slot):
        return remote(
            gl_out.at[to_slot], gl_in.at[slot], gl_send.at[to_slot], gl_recv.at[slot], to
        )

    for load in loads:
        load.wait()
    right = jnp.where(causal, right_ref[...].astype(F32), 0.0)
    rights[0] = right.astype(BF16)
    rights[1] = right.T.astype(BF16)
    for c in range(parts):
        compute_a(c)
    gram[...] = jnp.zeros_like(gram)
    term[...] = jnp.zeros_like(term)
    eye = (iota((rows, rows), 0) == iota((rows, rows), 1)).astype(BF16)
    left_out[...] = dot(left_ref[...], eye, ((0,), (0,))).astype(BF16)
    pl.semaphore_wait(barrier, n - 1)
    send_a(0)
    for plane in range(PLANES):
        to = PEERS * plane + z

        @pl.when(to != me)
        def _(to=to):
            left_copy(to, i).start()

        @pl.when(to == me)
        def _():
            left_in[i] = left_out[...]

    for c in range(1, min(AHEAD, parts)):
        send_a(c)
    start_relays(0)

    size = n * jj

    def pick():
        row, col = iota((size, size), 0), iota((size, size), 1)
        return col == (row % jj) * n + row // jj

    def spread():
        return iota((n, size), 1) // jj == iota((n, size), 0)

    def keep():
        row, col = iota((size, size), 0), iota((size, size), 1)
        return (row % jj == col % jj) & (row // jj >= col // jj)

    for s in range(PEERS):
        src = PEERS * i + s

        @pl.when(src != me)
        def _(src=src, s=s):
            left_copy(src, s).wait_recv()

    left_all = jnp.concatenate([left_in[s] for s in range(PEERS)], axis=1)
    picked = dot(pick().astype(BF16), left_all, ((1,), (1,))).astype(BF16)
    weights[...] = jnp.where(keep(), dot(picked, spread().astype(BF16)), 0.0).astype(BF16)
    weights_t[...] = weights[...].T

    def left_grads():
        best = lax.Precision.HIGHEST
        summed = dot(
            jnp.where(keep(), gram[...], 0.0), spread().astype(F32), ((1,), (1,)), precision=best
        )
        flat = dot(summed, pick().astype(F32), ((0,), (0,)), precision=best)
        each = size // PEERS
        for s in range(PEERS):
            gl_out[s] = flat[:, s * each : (s + 1) * each]
            to = PEERS * i + s

            @pl.when(to != me)
            def _(to=to, s=s):
                gl_copy(s, to, z).start()

            @pl.when(to == me)
            def _(s=s):
                gl_in[z] = gl_out[s]

    def at(cond, stage, c):
        @pl.when(cond)
        def _():
            stage(c)

    @pl.loop(0, parts + 3)
    def _(t):
        at(t < parts - AHEAD, send_a, t + AHEAD)
        at(t < parts - 1, start_relays, t + 1)
        at(t < parts, stage_b, t)
        at((t >= 1) & (t <= parts), stage_d, t - 1)
        at((t >= 2) & (t <= parts + 1), stage_s, t - 2)

        @pl.when(t == parts)
        def _():
            left_grads()

        at(t >= 3, stage_e, t - 3)

    for plane in range(PLANES):
        src = PEERS * plane + z

        @pl.when(src != me)
        def _(src=src, plane=plane):
            gl_copy(0, src, plane).wait_recv()

    total = gl_in[0] + gl_in[1] + gl_in[2] + gl_in[3]
    gleft_ref[...] = total.T

    @pl.loop(1, n)
    def _(k):
        src = lax.rem(me + n - k, n)
        term_copy(src, src).wait_recv()

    term_in[me] = term_out[me]
    gright_ref[...] = jnp.sum(term_in[...], axis=0)

    @pl.loop(0, parts)
    def _(c):
        for k in range(1, PEERS):
            p = lax.rem(i + k, PEERS)
            for kind in range(2):
                a_copy(kind, c, p).wait_send()
                b_copy(kind, c, p, i).wait_send()
        for q, (kind, targets) in relays.items():

            @pl.when(z == q)
            def _(q=q, kind=kind, targets=targets):
                for slot, to_plane in enumerate(targets):
                    relay(kind, c, q, slot, to_plane).wait_send()

        @pl.when((z == 1) | (z == 2))
        def _():
            sums(c, 0).wait_send()

    for plane in range(PLANES):
        to = PEERS * plane + z

        @pl.when(to != me)
        def _(to=to):
            left_copy(to, i).wait_send()

    for s in range(PEERS):
        to = PEERS * i + s

        @pl.when(to != me)
        def _(to=to, s=s):
            gl_copy(s, to, z).wait_send()

    @pl.loop(1, n)
    def _(k):
        term_copy(lax.rem(me + k, n), me).wait_send()


def fused_shards(parts, inputs, gate_in, grad_out, right_factor, left_factor):
    rows, width = inputs.shape
    n = PLANES * PEERS
    r, jj, w = rows // n, rows // PEERS, width // parts
    left2 = left_factor.reshape(r * n, n)
    vmem = pl.BlockSpec(memory_space=pltpu.VMEM)
    hbm = pl.BlockSpec(memory_space=pl.ANY)
    dma = pltpu.SemaphoreType.DMA
    gx, gg, gr, gl = pl.pallas_call(
        functools.partial(kernel, parts),
        out_shape=(
            jax.ShapeDtypeStruct(inputs.shape, BF16),
            jax.ShapeDtypeStruct(inputs.shape, BF16),
            jax.ShapeDtypeStruct((r, rows), F32),
            jax.ShapeDtypeStruct((r * n, n), F32),
        ),
        in_specs=[hbm] * 5,
        out_specs=(vmem,) * 4,
        scratch_shapes=[
            pltpu.VMEM(inputs.shape, BF16),
            pltpu.VMEM(inputs.shape, BF16),
            pltpu.VMEM(inputs.shape, BF16),
            pltpu.VMEM(right_factor.shape, BF16),
            pltpu.VMEM(left2.shape, BF16),
            pltpu.VMEM((2, parts, PEERS, jj, w), BF16),
            pltpu.VMEM((2, parts, n, jj, w), BF16),
            pltpu.VMEM((2, parts, PEERS, jj, w), BF16),
            pltpu.VMEM((2, parts, PEERS, jj, w), BF16),
            pltpu.VMEM((parts, PEERS, jj, w), SUMS),
            pltpu.VMEM((parts, PEERS, jj, w), SUMS),
            pltpu.VMEM((n * jj, n * jj), BF16),
            pltpu.VMEM((n * jj, n * jj), BF16),
            pltpu.VMEM((2, rows, rows), BF16),
            pltpu.VMEM((n * jj, n * jj), F32),
            pltpu.VMEM((rows, rows), F32),
            pltpu.VMEM((n, r * n), BF16),
            pltpu.VMEM((PEERS, n, r * n), BF16),
            pltpu.VMEM((PEERS, n, r * n), F32),
            pltpu.VMEM((PLANES, n, r * n), F32),
            pltpu.VMEM((n, r, rows), F32),
            pltpu.VMEM((n, r, rows), F32),
            dma((5,)),
            dma((2, parts, PEERS)),
            dma((2, parts, PEERS)),
            dma((parts, 2)),
            dma((2, parts, PLANES)),
            dma((parts,)),
            dma((parts,)),
            dma((2, parts, PEERS)),
            dma((2, parts, PEERS)),
            dma((PLANES,)),
            dma((PEERS,)),
            dma((PEERS,)),
            dma((PLANES,)),
            dma((n,)),
            dma((n,)),
        ],
        compiler_params=pltpu.CompilerParams(
            collective_id=0, has_side_effects=True, vmem_limit_bytes=56 * 2**20
        ),
    )(inputs, gate_in, grad_out, right_factor, left2)
    return gx, gg, gr, gl.reshape(r, n, n)


def solution(mesh):
    n = mesh.shape["seqa"]

    def shards(inputs, gate_in, grad_out, right_factor, left_factor):
        rows = inputs.shape[0]
        if n == PLANES * PEERS and rows == 128 and left_factor.shape == (8, n, n):
            return fused_shards(PARTS, inputs, gate_in, grad_out, right_factor, left_factor)
        return plain_shards(inputs, gate_in, grad_out, right_factor, left_factor)

    in_specs = (
        P(("groups", "seqa"), None),
        P(("groups", "seqa"), None),
        P(("groups", "seqa"), None),
        P(),
        P("seqa", None, None),
    )
    out_specs = (
        P(("groups", "seqa"), None),
        P(("groups", "seqa"), None),
        P(("groups", "seqa"), None),
        P(("groups", "seqa"), None, None),
    )
    return jax.shard_map(shards, mesh=mesh, in_specs=in_specs, out_specs=out_specs, check_vma=False)
```

```python
import functools

import jax
import jax.numpy as jnp
from jax import lax
from jax.experimental import pallas as pl
from jax.experimental.pallas import tpu as pltpu
from jax.sharding import PartitionSpec as P

F32, BF16 = jnp.float32, jnp.bfloat16
PARTS = 8
SUMS = BF16


def gate_grads(mixed, gate_in, grad_out):
    gate_f = gate_in.astype(jnp.float32)
    grad_f = grad_out.astype(jnp.float32)
    sig = jax.nn.sigmoid(gate_f)
    grad_mixed = (grad_f * gate_f * sig).astype(jnp.bfloat16)
    grad_gate = (grad_f * mixed.astype(jnp.float32) * sig * (1.0 + gate_f * (1.0 - sig))).astype(
        jnp.bfloat16
    )
    return (grad_mixed, grad_gate)


def plain_shards(inputs, gate_in, grad_out, right_factor, left_factor):
    places = jnp.arange(right_factor.shape[0])
    mask_right = (places[:, None] >= places[None, :]).astype(right_factor.dtype)
    right_masked = right_factor * mask_right
    blocks = jnp.arange(left_factor.shape[1])
    mask_left = (blocks[:, None] >= blocks[None, :]).astype(left_factor.dtype)
    left_masked = left_factor * mask_left[None]
    first = jnp.dot(right_masked, inputs, preferred_element_type=jnp.float32).astype(jnp.bfloat16)
    first_cols = lax.all_to_all(first[None], "seqa", split_axis=1, concat_axis=0, tiled=True)
    second = jnp.einsum(
        "jpa,ajd->pjd", left_masked, first_cols, preferred_element_type=jnp.float32
    ).astype(jnp.bfloat16)
    mixed = lax.all_to_all(second, "seqa", split_axis=0, concat_axis=1, tiled=True)[0]
    grad_mixed, grad_gate = gate_grads(mixed, gate_in, grad_out)
    grad_cols = lax.all_to_all(grad_mixed[None], "seqa", split_axis=1, concat_axis=0, tiled=True)
    grad_first_cols = jnp.einsum(
        "jpa,pjd->ajd", left_masked, grad_cols, preferred_element_type=jnp.float32
    ).astype(jnp.bfloat16)
    grad_left = jnp.einsum(
        "pjd,ajd->jpa", grad_cols, first_cols, preferred_element_type=jnp.float32
    ) * mask_left[None].astype(jnp.float32)
    grad_first = lax.all_to_all(grad_first_cols, "seqa", split_axis=0, concat_axis=1, tiled=True)[0]
    grad_inputs = jnp.dot(right_masked.T, grad_first, preferred_element_type=jnp.float32).astype(
        jnp.bfloat16
    )
    mask_float = mask_right.astype(jnp.float32)
    term = lax.dot_general(
        grad_first, inputs, (((1,), (1,)), ((), ())), preferred_element_type=jnp.float32
    )
    grad_right = lax.psum_scatter(term * mask_float, "seqa", scatter_dimension=0, tiled=True)
    return (grad_inputs, grad_gate, grad_right, grad_left)


AHEAD = 2


def iota(shape, dim):
    return lax.broadcasted_iota(jnp.int32, shape, dim)


def dot(a, b, dims=((1,), (0,)), **kw):
    return lax.dot_general(a, b, (dims, ((), ())), preferred_element_type=F32, **kw)


PLANES = 4
PEERS = 4


def kernel(
    parts, x_hbm, gate_hbm, gout_hbm, right_hbm, left_hbm,
    gx_ref, ggate_ref, gright_ref, gleft_ref,
    x_ref, gate_ref, gout_ref, right_ref, left_ref,
    cols_out, cols, back_out, back_in, sums_out, sums_in, weights, weights_t, rights, gram, term,
    left_out, left_in, gl_out, gl_in, term_out, term_in,
    load_sem, a_send, a_recv, relay_send, relay_recv, sum_send, sum_recv, b_send, b_recv,
    left_send, left_recv, gl_send, gl_recv, t_send, t_recv,
):
    n = PLANES * PEERS
    me = lax.axis_index("seqa")
    z, i = me // PEERS, me % PEERS
    rows, width = x_ref.shape
    jj = rows // PEERS
    w = width // parts
    m = PEERS * jj
    barrier = pltpu.get_barrier_semaphore()

    def remote(src, dst, send, recv, to):
        return pltpu.make_async_remote_copy(
            src_ref=src, dst_ref=dst, send_sem=send, recv_sem=recv,
            device_id={"seqa": to}, device_id_type=pl.DeviceIdType.MESH,
        )

    @pl.loop(1, n)
    def _(k):
        pl.semaphore_signal(
            barrier, inc=1, device_id={"seqa": lax.rem(me + k, n)},
            device_id_type=pl.DeviceIdType.MESH,
        )

    pairs = (
        (x_hbm, x_ref), (right_hbm, right_ref), (gate_hbm, gate_ref),
        (gout_hbm, gout_ref), (left_hbm, left_ref),
    )
    loads = [pltpu.make_async_copy(a, b, load_sem.at[k]) for k, (a, b) in enumerate(pairs)]
    for load in loads:
        load.start()

    def columns(c):
        return pl.ds(pl.multiple_of(c * w, w), w)

    causal = iota((rows, rows), 0) >= iota((rows, rows), 1)


    def block(kind, c, q):
        return cols.at[kind, c, pl.ds(PEERS * q, PEERS)]

    def planes(kind, c, lo, hi):
        return cols[kind, c, PEERS * lo : PEERS * hi].reshape((hi - lo) * m, w)

    def wt_block(q0, q1, p0, p1):
        return weights_t[m * q0 : m * q1, m * p0 : m * p1]

    def w_block(p0, p1, q0, q1):
        return weights[m * p0 : m * p1, m * q0 : m * q1]

    def a_copy(kind, c, p):
        return remote(
            cols_out.at[kind, c, p], cols.at[kind, c, me],
            a_send.at[kind, c, p], a_recv.at[kind, c, i], PEERS * z + p,
        )

    def a_arrival(kind, c, p):
        return remote(
            cols_out.at[kind, c, p], cols.at[kind, c, PEERS * z + p],
            a_send.at[kind, c, p], a_recv.at[kind, c, p], PEERS * z + p,
        )

    def compute_a(c):
        first = dot(rights[0], x_ref[:, columns(c)])
        cols_out[0, c] = first.astype(BF16).reshape(PEERS, jj, w)
        gate = gate_ref[:, columns(c)].astype(F32)
        gout = gout_ref[:, columns(c)].astype(F32)
        mixed_grad = gout * gate * jax.nn.sigmoid(gate)
        cols_out[1, c] = mixed_grad.astype(BF16).reshape(PEERS, jj, w)
        for kind in range(2):
            cols[kind, c, me] = cols_out[kind, c, i]

    def send_a(c):
        for k in range(1, PEERS):
            for kind in range(2):
                a_copy(kind, c, lax.rem(i + k, PEERS)).start()

    relays = {0: (0, (2, 1)), 1: (0, (2,)), 2: (1, (1,)), 3: (1, (1, 2))}

    def relay(kind, c, q, slot, to_plane):
        return remote(
            block(kind, c, q), block(kind, c, q),
            relay_send.at[c, slot], relay_recv.at[kind, c, q], PEERS * to_plane + i,
        )

    def sums(c, to_plane):
        return remote(
            sums_out.at[c], sums_in.at[c], sum_send.at[c], sum_recv.at[c], PEERS * to_plane + i
        )

    def b_copy(kind, c, p, slot):
        return remote(
            back_out.at[kind, c, p], back_in.at[kind, c, slot],
            b_send.at[kind, c, p], b_recv.at[kind, c, slot], PEERS * z + p,
        )

    def send_back(kind, c, value):
        back_out[kind, c] = value.astype(BF16).reshape(PEERS, jj, w)
        for k in range(1, PEERS):
            b_copy(kind, c, lax.rem(i + k, PEERS), i).start()
        back_in[kind, c, i] = back_out[kind, c, i]

    def add_gram(c, p0, p1, q0, q1):
        gram[m * p0 : m * p1, m * q0 : m * q1] += dot(
            planes(1, c, p0, p1), planes(0, c, q0, q1), ((1,), (1,))
        )

    def start_relays(c):
        for k in range(1, PEERS):
            for kind in range(2):
                a_arrival(kind, c, lax.rem(i + PEERS - k, PEERS)).wait_recv()
        for q, (kind, targets) in relays.items():

            @pl.when(z == q)
            def _(q=q, kind=kind, targets=targets):
                for slot, to_plane in enumerate(targets):
                    relay(kind, c, q, slot, to_plane).start()

    def stage_b(c):
        @pl.when(z == 0)
        def _():
            send_back(0, c, dot(w_block(0, 1, 0, 1), planes(0, c, 0, 1)))
            add_gram(c, 0, 1, 0, 1)

        @pl.when(z == 3)
        def _():
            send_back(1, c, dot(wt_block(3, 4, 3, 4), planes(1, c, 3, 4)))
            add_gram(c, 3, 4, 3, 4)

    def stage_d(c):
        @pl.when(z == 1)
        def _():
            relay(0, c, 0, 0, 0).wait_recv()
            send_back(0, c, dot(w_block(1, 2, 0, 2), planes(0, c, 0, 2)))
            relay(1, c, 2, 0, 2).wait_recv()
            relay(1, c, 3, 0, 3).wait_recv()
            g = planes(1, c, 1, 4)
            summed = dot(wt_block(0, 1, 1, 4), g)
            sums_out[c] = summed.astype(SUMS).reshape(PEERS, jj, w)
            sums(c, 0).start()
            send_back(1, c, dot(wt_block(1, 2, 1, 4), g))
            add_gram(c, 1, 4, 0, 1)
            add_gram(c, 1, 2, 1, 2)

        @pl.when(z == 2)
        def _():
            relay(1, c, 3, 0, 3).wait_recv()
            send_back(1, c, dot(wt_block(2, 3, 2, 4), planes(1, c, 2, 4)))
            relay(0, c, 1, 0, 1).wait_recv()
            relay(0, c, 0, 0, 0).wait_recv()
            f = planes(0, c, 0, 3)
            sums_out[c] = dot(w_block(3, 4, 0, 3), f).astype(SUMS).reshape(PEERS, jj, w)
            sums(c, 3).start()
            send_back(0, c, dot(w_block(2, 3, 0, 3), f))
            add_gram(c, 2, 4, 1, 3)

    def stage_s(c):
        @pl.when(z == 0)
        def _():
            own = dot(wt_block(0, 1, 0, 1), planes(1, c, 0, 1))
            sums(c, 1).wait_recv()
            send_back(1, c, own + sums_in[c].reshape(m, w))

        @pl.when(z == 3)
        def _():
            own = dot(w_block(3, 4, 3, 4), planes(0, c, 3, 4))
            sums(c, 2).wait_recv()
            send_back(0, c, own + sums_in[c].reshape(m, w))

    def term_copy(to, slot):
        return remote(term_out.at[to], term_in.at[slot], t_send.at[to], t_recv.at[slot], to)

    def stage_e(c):
        for k in range(1, PEERS):
            p = lax.rem(i + PEERS - k, PEERS)
            for kind in range(2):
                b_copy(kind, c, p, p).wait_recv()
        grad_first = back_in[1, c].reshape(rows, w)
        term[...] += dot(grad_first, x_ref[:, columns(c)], ((1,), (1,)))

        @pl.when(c == parts - 1)
        def _():
            term_out[...] = jnp.where(causal, term[...], 0.0).reshape(n, rows // n, rows)

            @pl.loop(1, n)
            def _(k):
                term_copy(lax.rem(me + k, n), me).start()

        gx_ref[:, columns(c)] = dot(rights[1], grad_first).astype(BF16)
        mixed = back_in[0, c].reshape(rows, w).astype(F32)
        gate = gate_ref[:, columns(c)].astype(F32)
        gout = gout_ref[:, columns(c)].astype(F32)
        sig = jax.nn.sigmoid(gate)
        ggate_ref[:, columns(c)] = (gout * mixed * sig * (1.0 + gate * (1.0 - sig))).astype(BF16)

    def left_copy(to, slot):
        return remote(left_out, left_in.at[slot], left_send.at[to // PEERS], left_recv.at[slot], to)

    def gl_copy(to_slot, to, slot):
        return remote(
            gl_out.at[to_slot], gl_in.at[slot], gl_send.at[to_slot], gl_recv.at[slot], to
        )

    for load in loads:
        load.wait()
    right = jnp.where(causal, right_ref[...].astype(F32), 0.0)
    rights[0] = right.astype(BF16)
    rights[1] = right.T.astype(BF16)
    for c in range(parts):
        compute_a(c)
    gram[...] = jnp.zeros_like(gram)
    term[...] = jnp.zeros_like(term)
    eye = (iota((rows, rows), 0) == iota((rows, rows), 1)).astype(BF16)
    left_out[...] = dot(left_ref[...], eye, ((0,), (0,))).astype(BF16)
    pl.semaphore_wait(barrier, n - 1)
    send_a(0)
    for plane in range(PLANES):
        to = PEERS * plane + z

        @pl.when(to != me)
        def _(to=to):
            left_copy(to, i).start()

        @pl.when(to == me)
        def _():
            left_in[i] = left_out[...]

    for c in range(1, min(AHEAD, parts)):
        send_a(c)
    start_relays(0)

    size = n * jj

    def pick():
        row, col = iota((size, size), 0), iota((size, size), 1)
        return col == (row % jj) * n + row // jj

    def spread():
        return iota((n, size), 1) // jj == iota((n, size), 0)

    def keep():
        row, col = iota((size, size), 0), iota((size, size), 1)
        return (row % jj == col % jj) & (row // jj >= col // jj)

    for s in range(PEERS):
        src = PEERS * i + s

        @pl.when(src != me)
        def _(src=src, s=s):
            left_copy(src, s).wait_recv()

    left_all = jnp.concatenate([left_in[s] for s in range(PEERS)], axis=1)
    picked = dot(pick().astype(BF16), left_all, ((1,), (1,))).astype(BF16)
    weights[...] = jnp.where(keep(), dot(picked, spread().astype(BF16)), 0.0).astype(BF16)
    weights_t[...] = weights[...].T

    def left_grads():
        best = lax.Precision.HIGHEST
        summed = dot(
            jnp.where(keep(), gram[...], 0.0), spread().astype(F32), ((1,), (1,)), precision=best
        )
        flat = dot(summed, pick().astype(F32), ((0,), (0,)), precision=best)
        each = size // PEERS
        for s in range(PEERS):
            gl_out[s] = flat[:, s * each : (s + 1) * each]
            to = PEERS * i + s

            @pl.when(to != me)
            def _(to=to, s=s):
                gl_copy(s, to, z).start()

            @pl.when(to == me)
            def _(s=s):
                gl_in[z] = gl_out[s]

    def at(cond, stage, c):
        @pl.when(cond)
        def _():
            stage(c)

    @pl.loop(0, parts + 3)
    def _(t):
        at(t < parts - AHEAD, send_a, t + AHEAD)
        at(t < parts - 1, start_relays, t + 1)
        at(t < parts, stage_b, t)
        at((t >= 1) & (t <= parts), stage_d, t - 1)
        at((t >= 2) & (t <= parts + 1), stage_s, t - 2)

        @pl.when(t == parts + 1)
        def _():
            left_grads()

        at(t >= 3, stage_e, t - 3)

    for plane in range(PLANES):
        src = PEERS * plane + z

        @pl.when(src != me)
        def _(src=src, plane=plane):
            gl_copy(0, src, plane).wait_recv()

    total = gl_in[0] + gl_in[1] + gl_in[2] + gl_in[3]
    gleft_ref[...] = total.T

    @pl.loop(1, n)
    def _(k):
        src = lax.rem(me + n - k, n)
        term_copy(src, src).wait_recv()

    term_in[me] = term_out[me]
    gright_ref[...] = jnp.sum(term_in[...], axis=0)

    @pl.loop(0, parts)
    def _(c):
        for k in range(1, PEERS):
            p = lax.rem(i + k, PEERS)
            for kind in range(2):
                a_copy(kind, c, p).wait_send()
                b_copy(kind, c, p, i).wait_send()
        for q, (kind, targets) in relays.items():

            @pl.when(z == q)
            def _(q=q, kind=kind, targets=targets):
                for slot, to_plane in enumerate(targets):
                    relay(kind, c, q, slot, to_plane).wait_send()

        @pl.when((z == 1) | (z == 2))
        def _():
            sums(c, 0).wait_send()

    for plane in range(PLANES):
        to = PEERS * plane + z

        @pl.when(to != me)
        def _(to=to):
            left_copy(to, i).wait_send()

    for s in range(PEERS):
        to = PEERS * i + s

        @pl.when(to != me)
        def _(to=to, s=s):
            gl_copy(s, to, z).wait_send()

    @pl.loop(1, n)
    def _(k):
        term_copy(lax.rem(me + k, n), me).wait_send()


def fused_shards(parts, inputs, gate_in, grad_out, right_factor, left_factor):
    rows, width = inputs.shape
    n = PLANES * PEERS
    r, jj, w = rows // n, rows // PEERS, width // parts
    left2 = left_factor.reshape(r * n, n)
    vmem = pl.BlockSpec(memory_space=pltpu.VMEM)
    hbm = pl.BlockSpec(memory_space=pl.ANY)
    dma = pltpu.SemaphoreType.DMA
    gx, gg, gr, gl = pl.pallas_call(
        functools.partial(kernel, parts),
        out_shape=(
            jax.ShapeDtypeStruct(inputs.shape, BF16),
            jax.ShapeDtypeStruct(inputs.shape, BF16),
            jax.ShapeDtypeStruct((r, rows), F32),
            jax.ShapeDtypeStruct((r * n, n), F32),
        ),
        in_specs=[hbm] * 5,
        out_specs=(vmem,) * 4,
        scratch_shapes=[
            pltpu.VMEM(inputs.shape, BF16),
            pltpu.VMEM(inputs.shape, BF16),
            pltpu.VMEM(inputs.shape, BF16),
            pltpu.VMEM(right_factor.shape, BF16),
            pltpu.VMEM(left2.shape, BF16),
            pltpu.VMEM((2, parts, PEERS, jj, w), BF16),
            pltpu.VMEM((2, parts, n, jj, w), BF16),
            pltpu.VMEM((2, parts, PEERS, jj, w), BF16),
            pltpu.VMEM((2, parts, PEERS, jj, w), BF16),
            pltpu.VMEM((parts, PEERS, jj, w), SUMS),
            pltpu.VMEM((parts, PEERS, jj, w), SUMS),
            pltpu.VMEM((n * jj, n * jj), BF16),
            pltpu.VMEM((n * jj, n * jj), BF16),
            pltpu.VMEM((2, rows, rows), BF16),
            pltpu.VMEM((n * jj, n * jj), F32),
            pltpu.VMEM((rows, rows), F32),
            pltpu.VMEM((n, r * n), BF16),
            pltpu.VMEM((PEERS, n, r * n), BF16),
            pltpu.VMEM((PEERS, n, r * n), F32),
            pltpu.VMEM((PLANES, n, r * n), F32),
            pltpu.VMEM((n, r, rows), F32),
            pltpu.VMEM((n, r, rows), F32),
            dma((5,)),
            dma((2, parts, PEERS)),
            dma((2, parts, PEERS)),
            dma((parts, 2)),
            dma((2, parts, PLANES)),
            dma((parts,)),
            dma((parts,)),
            dma((2, parts, PEERS)),
            dma((2, parts, PEERS)),
            dma((PLANES,)),
            dma((PEERS,)),
            dma((PEERS,)),
            dma((PLANES,)),
            dma((n,)),
            dma((n,)),
        ],
        compiler_params=pltpu.CompilerParams(
            collective_id=0, has_side_effects=True, vmem_limit_bytes=56 * 2**20
        ),
    )(inputs, gate_in, grad_out, right_factor, left2)
    return gx, gg, gr, gl.reshape(r, n, n)


def solution(mesh):
    n = mesh.shape["seqa"]

    def shards(inputs, gate_in, grad_out, right_factor, left_factor):
        rows = inputs.shape[0]
        if n == PLANES * PEERS and rows == 128 and left_factor.shape == (8, n, n):
            return fused_shards(PARTS, inputs, gate_in, grad_out, right_factor, left_factor)
        return plain_shards(inputs, gate_in, grad_out, right_factor, left_factor)

    in_specs = (
        P(("groups", "seqa"), None),
        P(("groups", "seqa"), None),
        P(("groups", "seqa"), None),
        P(),
        P("seqa", None, None),
    )
    out_specs = (
        P(("groups", "seqa"), None),
        P(("groups", "seqa"), None),
        P(("groups", "seqa"), None),
        P(("groups", "seqa"), None, None),
    )
    return jax.shard_map(shards, mesh=mesh, in_specs=in_specs, out_specs=out_specs, check_vma=False)
```
